32 devices in a mesh: grp: 1, node: 2 (over core), local: 16 (over z, y, x).
Axes of the slice: x: 2, y: 2, z: 4, core: 2. Of those that a mesh axis runs over, the one named last changes fastest.
Arguments:
- tokens: bfloat16 [2048, 7168], P(('grp', 'node', 'local')), may hold values from -6 to 6
- expert_ids: int32 [2048, 2], P(('grp', 'node', 'local')), may hold values from 0 to 3, all different within a row; in each aligned block of 64 rows (0 to 63, 64 to 127, ...) at most 40 rows name the same one
- scores: float32 [2048, 2], P(('grp', 'node', 'local')), may hold values from 0.05 to 1
- w_gate: bfloat16 [7168, 8192], P(None, ('node', 'local')), may hold values from -0.0625 to 0.0625
- w_up: bfloat16 [7168, 8192], P(None, ('node', 'local')), may hold values from -0.0625 to 0.0625
- w_down: bfloat16 [32, 2048, 896], P(('node', 'local')), may hold values from -0.125 to 0.125
Outputs:
- mixed: bfloat16 [2048, 7168], P(('grp', 'node', 'local'))
The draws below stay inside these ranges and needn't reach their ends.
Inputs may be any that keep to these rules, and one draw needn't show every extreme that they name: `expert_ids`: each row names 2 different experts and every expert is named by some row; within the rows of one device no expert is named by more than 40 rows, a bound that some block reaches.
All inputs are finite; a program needn't handle non-finite values.
Results may differ from the reference program's by a relative error of at most 0.0059.
Values may be sent and summed in bfloat16 or wider, within the bound.
A program may use at most 192 MiB of HBM per device.

```python
import math
import jax
import jax.numpy as jnp
import numpy as np
from jax import lax

D = 7168
FF = 2048
SPLIT = 8
TOK_DEV = 64
EXPERTS = 4
TOP = 2
CAP = 40
TOKENS = 2048
N_NODE = 2
N_LOCAL = 16


def block_scale(rng, shape, shards, low, top_value):
    def one(dim, parts):
        steps = jax.random.uniform(jax.random.fold_in(jax.random.fold_in(rng, 6), dim), (parts,), jnp.float32, low / len(shards), top_value / len(shards))
        return jnp.repeat(jnp.exp(steps), shape[dim] // parts).reshape((-1,) + (1,) * (len(shape) - dim - 1))

    factor_of = one(*shards[0])
    for cut in shards[1:]:
        factor_of = factor_of * one(*cut)
    return factor_of


def routed_block(key, own, number, rows, amount, top, bound, lean):
    sequence = jax.random.permutation(key, amount)
    heavy_load, ordinary = portions_of(amount, rows * top, bound, lean, True), portions_of(amount, rows * top, bound, lean, False)
    places = jnp.arange(amount)

    def named(lengths, offset_by):
        used = int((lengths > 0).sum())
        fixed = max(1, used // 4)
        passed = fixed + (places - fixed + offset_by * (used - fixed)) % max(1, amount - fixed)
        return jnp.zeros((amount,), jnp.int32).at[sequence[jnp.where(places < fixed, places, passed)]].set(jnp.asarray(lengths, jnp.int32))

    lengths = jnp.where(number % 4 == 0, named(heavy_load, number // 4), named(ordinary, number - number // 4 - 1))
    mixed = jax.random.permutation(jax.random.fold_in(own, 3), amount)
    giver, sink = mixed[0:amount // 2 * 2:2], mixed[1:amount // 2 * 2:2]
    margin = jnp.minimum(lengths[giver] - 1, bound - lengths[sink]) // 2
    margin = jnp.where((giver == sequence[0]) | (sink == sequence[0]) | (lengths[sink] == 0), 0, jnp.maximum(margin, 0))
    passed = jax.random.randint(jax.random.fold_in(own, 4), (amount // 2,), 0, 1 << 20) % (margin + 1)
    lengths = lengths.at[giver].add(-passed).at[sink].add(passed)
    items = jnp.searchsorted(jnp.cumsum(lengths), jnp.arange(rows * top), side="right").astype(jnp.int32)
    grid = items.reshape(top, rows).T
    grid = grid[jax.random.permutation(jax.random.fold_in(own, 1), rows)]
    offset_by = jax.random.randint(jax.random.fold_in(own, 2), (rows, 1), 0, top)
    return jnp.take_along_axis(grid, (jnp.arange(top)[None, :] + offset_by) % top, axis=1)


def portions_of(count, total, limit, skew, full):
    loads = [(1 << 20) // math.isqrt(grade ** skew) + 1 for grade in range(1, count + 1)]
    largest = limit if full else min(limit, max(-(-total // count), total * loads[0] // sum(loads)))
    least = 1 if total - largest >= count - 1 else 0
    counts, rest = [largest] + [least] * (count - 1), total - largest - least * (count - 1)
    while rest > 0:
        movable = [i for i in range(1, count) if counts[i] < largest] or [i for i in range(1, count) if counts[i] < limit]
        mass, remaining = sum([loads[i] for i in movable]), rest
        for i in movable:
            addition = min(limit - counts[i], max(1, remaining * loads[i] // mass), rest)
            counts[i] = counts[i] + addition
            rest = rest - addition
    return np.array(counts)


def centred(key, extent, deviation, reach, split=(), kind=jnp.bfloat16):
    loudness = block_scale(key, extent, split, -0.22, 0.18) if split else 1.0
    drawn = jax.random.normal(key, extent, jnp.float32) * deviation * loudness
    return jnp.minimum(jnp.maximum(drawn, -reach), reach).astype(kind)


def setup_inputs(seed: int = 0, part: int = 0) -> dict:
    key_of = jax.random.split(jax.random.key(seed), 7)
    own_keys = jax.random.split(jax.random.fold_in(key_of[6], part), 7)
    tokens = centred(own_keys[0], (TOKENS, D), 1.0, 6.0, ((0, 32),))
    expert_ids_keys = jax.random.split(jax.random.fold_in(own_keys[1], 1), TOKENS // TOK_DEV)
    expert_ids_turns = jax.random.permutation(jax.random.fold_in(own_keys[1], 3), TOKENS // TOK_DEV)
    expert_ids = jax.vmap(lambda own, number: routed_block(jax.random.fold_in(own_keys[1], 2), own, number, TOK_DEV, EXPERTS, TOP, CAP, 2))(expert_ids_keys, expert_ids_turns).reshape((TOKENS, TOP))
    scores = jnp.clip(jnp.exp(math.log(1.0) - 2.9957323 * jax.random.uniform(own_keys[2], (TOKENS, TOP), jnp.float32) ** block_scale(own_keys[2], (TOKENS, TOP), ((0, 32),), -0.2, 0.2)), 0.05, 1.0)
    w_gate = centred(key_of[3], (D, EXPERTS * FF), D ** -0.5, 0.0625, ((1, 32),))
    w_up = centred(key_of[4], (D, EXPERTS * FF), D ** -0.5, 0.0625, ((1, 32),))
    w_down = centred(key_of[5], (EXPERTS * SPLIT, FF, D // SPLIT), FF ** -0.5, 0.125, ((0, 32),))
    return {"tokens": tokens, "expert_ids": expert_ids, "scores": scores, "w_gate": w_gate, "w_up": w_up, "w_down": w_down}


def reference(tokens, expert_ids, scores, w_gate, w_up, w_down):
    weights = 2.5 * scores / jnp.sum(scores, axis=1, keepdims=True)
    expert_range = jnp.arange(EXPERTS, dtype=jnp.int32)
    one_hot = (expert_ids[:, :, None] == expert_range[None, None, :])
    route_weight = jnp.sum(weights[:, :, None] * one_hot.astype(jnp.float32), axis=1).astype(jnp.bfloat16)
    named = jnp.sum(one_hot.astype(jnp.int32), axis=1).astype(jnp.int32)
    position = (jnp.cumsum(named, axis=0) - named).astype(jnp.int32)
    list_len = N_NODE * N_LOCAL * CAP
    position = jnp.where(named > 0, position, list_len).astype(jnp.int32)
    token_range = jnp.arange(TOKENS, dtype=jnp.int32)
    row_index = jnp.broadcast_to(token_range[:, None], (TOKENS, EXPERTS)).astype(jnp.int32)
    col_index = jnp.broadcast_to(expert_range[None, :], (TOKENS, EXPERTS)).astype(jnp.int32)
    table = jnp.full((EXPERTS, list_len), TOKENS, dtype=jnp.int32)
    table = table.at[col_index.reshape(-1), position.reshape(-1)].set(row_index.reshape(-1), mode="drop")

    def one_expert(running, expert_index):
        listed = table[expert_index]
        valid = (listed < TOKENS).astype(jnp.float32)
        safe = jnp.minimum(listed, TOKENS - 1).astype(jnp.int32)
        rows = tokens[safe]
        start_col = (expert_index * FF).astype(jnp.int32)
        gate_cols = lax.dynamic_slice_in_dim(w_gate, start_col, FF, 1)
        up_cols = lax.dynamic_slice_in_dim(w_up, start_col, FF, 1)
        blocks = lax.dynamic_slice_in_dim(w_down, (expert_index * SPLIT).astype(jnp.int32), SPLIT, 0)
        down_full = blocks.transpose(1, 0, 2).reshape(FF, D)
        gate_proj = jnp.dot(rows, gate_cols, preferred_element_type=jnp.float32)
        up_proj = jnp.dot(rows, up_cols, preferred_element_type=jnp.float32)
        coefficient = (route_weight[safe, expert_index].astype(jnp.float32) * valid)[:, None]
        hidden = (jax.nn.silu(gate_proj) * up_proj * coefficient).astype(jnp.bfloat16)
        result = jnp.dot(hidden, down_full, preferred_element_type=jnp.float32)
        return running.at[safe].add(result), None

    start_sum = jnp.zeros((TOKENS, D), jnp.float32)
    summed, unused = lax.scan(one_expert, start_sum, expert_range)
    return summed.astype(jnp.bfloat16)
```

```python
import jax
import jax.numpy as jnp
from jax import lax
from jax.sharding import PartitionSpec as P

SPLIT = 8


def on_device(tokens, expert_ids, scores, w_gate, w_up, w_down):
    rows, width = tokens.shape
    nodes, locals_ = lax.axis_size("node"), lax.axis_size("local")
    devices = nodes * locals_
    experts = devices // SPLIT
    halves = locals_ // SPLIT
    top = expert_ids.shape[1]
    cap = min(rows, max(2, rows * top * 5 // (experts * 4)))
    columns = w_down.shape[2]
    mine = lax.axis_index("node") * halves + lax.axis_index("local") // SPLIT

    weights = 2.5 * scores / jnp.sum(scores, axis=1, keepdims=True)
    hot = expert_ids[:, :, None] == jnp.arange(experts, dtype=jnp.int32)
    route = jnp.sum(jnp.where(hot, weights[:, :, None], 0.0), axis=1)
    route = lax.all_gather(route.astype(jnp.bfloat16), ("node", "local"), axis=0)
    route_mine = lax.dynamic_slice_in_dim(route, mine, 1, 2)[:, :, 0].astype(jnp.float32)
    named = route_mine > 0
    upto = jnp.cumsum(named.astype(jnp.int32), axis=1) - 1
    slot = jnp.where(named, upto, -1)
    pack = (slot[:, None, :] == jnp.arange(cap, dtype=jnp.int32)[None, :, None]).astype(jnp.bfloat16)

    gathered = lax.all_gather(tokens, "local", axis=0, tiled=True)
    gathered = lax.all_gather(gathered, "node", axis=0, tiled=True)
    gate = jnp.dot(gathered, w_gate, preferred_element_type=jnp.float32)
    up = jnp.dot(gathered, w_up, preferred_element_type=jnp.float32)
    hidden = (jax.nn.silu(gate) * up * route_mine.reshape(-1, 1)).astype(jnp.bfloat16)
    packed = jnp.einsum("sct,sth->sch", pack, hidden.reshape(devices, rows, -1),
                        preferred_element_type=jnp.float32).astype(jnp.bfloat16)
    groups = [list(range(h * SPLIT, (h + 1) * SPLIT)) for h in range(halves)]
    whole = lax.all_gather(packed, "local", axis=0, axis_index_groups=groups)
    spread = jnp.einsum("sct,fsch->stfh", pack, whole,
                        preferred_element_type=jnp.float32).astype(jnp.bfloat16)
    out = jnp.dot(spread.reshape(devices * rows, -1), w_down[0], preferred_element_type=jnp.float32)
    half = lax.psum_scatter(out, "node", scatter_dimension=0, tiled=True)
    half = half.astype(jnp.bfloat16).reshape(locals_, rows, columns)
    back = lax.all_to_all(half, "local", split_axis=0, concat_axis=0, tiled=True)
    back = back.astype(jnp.float32).reshape(halves, SPLIT, rows, columns)
    mixed = jnp.sum(back, axis=0)
    return mixed.transpose(1, 0, 2).reshape(rows, width).astype(jnp.bfloat16)


def solution(mesh):
    placed = (
        P(("grp", "node", "local"), None),
        P(("grp", "node", "local"), None),
        P(("grp", "node", "local"), None),
        P(None, ("node", "local")),
        P(None, ("node", "local")),
        P(("node", "local"), None, None),
    )
    return jax.shard_map(
        on_device,
        mesh=mesh,
        in_specs=placed,
        out_specs=P(("grp", "node", "local"), None),
        check_vma=False,
    )
```

```python
import jax
import jax.numpy as jnp
from jax import lax
from jax.experimental import pallas as pl
from jax.experimental.pallas import tpu as pltpu
from jax.sharding import PartitionSpec as P

SPLIT = 8
MESH = pl.DeviceIdType.MESH


def device(core, local):
    return {"node": core, "local": local}


def token_gather(lines, own_ref, all_ref, send_sem, recv_sem, own_sem):
    core, local = lax.axis_index("node"), lax.axis_index("local")
    count = lines * 4
    z, y, x = local // 4, local // 2 % 2, local % 2
    to_x, to_y = local + 1 - 2 * x, local + 2 - 4 * y
    first = (1 - core) * to_x + core * to_y
    second = core * to_x + (1 - core) * to_y
    below, above = local - 4, local + 4
    base, other = core * count, (1 - core) * count

    place = pltpu.make_async_copy(own_ref, all_ref.at[base + local], own_sem)
    place.start()
    barrier = pltpu.get_barrier_semaphore()
    for peer in (device(core, first), device(core, second), device(1 - core, local)):
        pl.semaphore_signal(barrier, inc=1, device_id=peer, device_id_type=MESH)

    @pl.when(z > 0)
    def _():
        pl.semaphore_signal(barrier, inc=1, device_id=device(core, below), device_id_type=MESH)

    @pl.when(z < lines - 1)
    def _():
        pl.semaphore_signal(barrier, inc=1, device_id=device(core, above), device_id_type=MESH)

    ends = (z + lines - 2) // (lines - 1) + (2 * lines - 3 - z) // (lines - 1)
    pl.semaphore_wait(barrier, 3 + ends)
    place.wait()

    def copy(source, kind, peer):
        return pltpu.make_async_remote_copy(
            src_ref=all_ref.at[base + source],
            dst_ref=all_ref.at[base + source],
            send_sem=send_sem.at[source, kind],
            recv_sem=recv_sem.at[base + source],
            device_id=peer,
            device_id_type=MESH,
        )

    def arrived(slot):
        pltpu.make_async_remote_copy(
            src_ref=all_ref.at[slot],
            dst_ref=all_ref.at[slot],
            send_sem=send_sem.at[0, 0],
            recv_sem=recv_sem.at[slot],
            device_id=device(1 - core, local),
            device_id_type=MESH,
        ).wait_recv()

    def up(source):
        return copy(source, 0, device(core, above))

    def down(source):
        return copy(source, 1, device(core, below))

    def to_second(source):
        return copy(source, 2, device(core, second))

    def to_first(source):
        return copy(source, 3, device(core, first))

    def to_core(source):
        return copy(source, 4, device(1 - core, local))

    def when(fits, action):
        @pl.when(fits)
        def _():
            action()

    def line(run):
        for step in range(lines):
            for sign in (-1, 1) if step else (0,):
                shift = sign * step
                fits = jnp.logical_and(z + shift >= 0, z + shift < lines)
                when(fits, lambda shift=shift, sign=sign: run(shift * 4, sign))

    def pass_on(shift, sign):
        source = local + shift
        if sign:
            arrived(base + source)
        if sign <= 0:
            when(z < lines - 1, lambda: up(source).start())
        if sign >= 0:
            when(z > 0, lambda: down(source).start())
        to_first(source).start()
        to_second(source).start()
        to_core(source).start()

    def pass_first(shift, sign):
        source = first + shift
        arrived(base + source)
        to_second(source).start()
        to_core(source).start()

    def pass_second(shift, sign, start):
        source = start + shift
        arrived(base + source)
        to_core(source).start()

    opposite = first + second - local
    steps = []
    for step in range(lines):
        for sign in (-1, 1) if step else (0,):
            steps.append((step, sign))
    for at in range(len(steps) + 2):
        for lag, run in (
            (0, pass_on),
            (1, pass_first),
            (2, lambda a, b: (pass_second(a, b, second), pass_second(a, b, opposite))),
        ):
            if 0 <= at - lag < len(steps):
                step, sign = steps[at - lag]
                shift = step * sign
                fits = jnp.logical_and(z + shift >= 0, z + shift < lines)
                when(fits, lambda run=run, shift=shift, sign=sign: run(shift * 4, sign))
    for source in range(count):
        arrived(other + source)

    def sent(shift, sign):
        source = local + shift
        if sign <= 0:
            when(z < lines - 1, lambda: up(source).wait_send())
        if sign >= 0:
            when(z > 0, lambda: down(source).wait_send())
        to_first(source).wait_send()
        to_second(source).wait_send()
        to_second(first + shift).wait_send()

    line(sent)
    for source in range(count):
        to_core(source).wait_send()


def hidden_gather(own_ref, all_ref, send_sem, recv_sem, own_sem):
    core, local = lax.axis_index("node"), lax.axis_index("local")
    rows, width = own_ref.shape
    third = -(-rows // 48) * 16
    cuts = [(0, third), (third, third), (2 * third, rows - 2 * third)]
    within = local % SPLIT
    flips = [(1 - 2 * (local // stride % 2)) * stride for stride in (1, 2, 4)]

    def block(index):
        return pl.ds(pl.multiple_of(index * width, width), width)

    place = pltpu.make_async_copy(own_ref, all_ref.at[:, block(within)], own_sem)
    place.start()
    barrier = pltpu.get_barrier_semaphore()
    for flip in flips:
        pl.semaphore_signal(barrier, inc=1, device_id=device(core, local + flip), device_id_type=MESH)
    pl.semaphore_wait(barrier, len(flips))
    place.wait()

    def copy(part, source, axis, peer):
        start, size = cuts[part]
        here = all_ref.at[pl.ds(start, size), block(source)]
        return pltpu.make_async_remote_copy(
            src_ref=here,
            dst_ref=here,
            send_sem=send_sem.at[part, axis, source],
            recv_sem=recv_sem.at[part, source],
            device_id=device(core, peer),
            device_id_type=MESH,
        )

    pending = []

    def send(part, source, axes):
        for axis in axes:
            moved = copy(part, source, axis, local + flips[axis])
            moved.start()
            pending.append(moved)

    orders = [[(part + turn) % 3 for turn in range(3)] for part in range(3)]
    held = [[within] for _ in range(3)]
    for part, order in enumerate(orders):
        send(part, within, order)
    for turn in range(3):
        for place_in in range(2**turn):
            for part, order in enumerate(orders):
                source = held[part][place_in] + flips[order[turn]]
                copy(part, source, 0, local + flips[order[turn]]).wait_recv()
                send(part, source, order[turn + 1 :])
                held[part].append(source)
    for moved in pending:
        moved.wait_send()


def gather_tokens(tokens, lines):
    rows, width = tokens.shape
    count = lines * 4
    return pl.pallas_call(
        lambda *refs: token_gather(lines, *refs),
        out_shape=jax.ShapeDtypeStruct((2 * count, rows, width), tokens.dtype),
        in_specs=[pl.BlockSpec(memory_space=pl.ANY)],
        out_specs=pl.BlockSpec(memory_space=pl.ANY),
        scratch_shapes=[
            pltpu.SemaphoreType.DMA((count, 5)),
            pltpu.SemaphoreType.DMA((2 * count,)),
            pltpu.SemaphoreType.DMA,
        ],
        compiler_params=pltpu.CompilerParams(collective_id=0, has_side_effects=True),
    )(tokens)


def gather_hidden(packed):
    rows, width = packed.shape
    return pl.pallas_call(
        hidden_gather,
        out_shape=jax.ShapeDtypeStruct((rows, SPLIT * width), packed.dtype),
        in_specs=[pl.BlockSpec(memory_space=pl.ANY)],
        out_specs=pl.BlockSpec(memory_space=pl.ANY),
        scratch_shapes=[
            pltpu.SemaphoreType.DMA((3, 3, SPLIT)),
            pltpu.SemaphoreType.DMA((3, SPLIT)),
            pltpu.SemaphoreType.DMA,
        ],
        compiler_params=pltpu.CompilerParams(collective_id=1, has_side_effects=True),
    )(packed)


def on_device(tokens, expert_ids, scores, w_gate, w_up, w_down):
    rows, width = tokens.shape
    nodes, locals_ = lax.axis_size("node"), lax.axis_size("local")
    devices = nodes * locals_
    experts = devices // SPLIT
    halves = locals_ // SPLIT
    top = expert_ids.shape[1]
    cap = min(rows, max(2, rows * top * 5 // (experts * 4)))
    columns = w_down.shape[2]
    mine = lax.axis_index("node") * halves + lax.axis_index("local") // SPLIT

    weights = 2.5 * scores / jnp.sum(scores, axis=1, keepdims=True)
    hot = expert_ids[:, :, None] == jnp.arange(experts, dtype=jnp.int32)
    route = jnp.sum(jnp.where(hot, weights[:, :, None], 0.0), axis=1)
    route = lax.all_gather(route.astype(jnp.bfloat16), ("node", "local"), axis=0)
    route_mine = lax.dynamic_slice_in_dim(route, mine, 1, 2)[:, :, 0].astype(jnp.float32)
    named = route_mine > 0
    upto = jnp.cumsum(named.astype(jnp.int32), axis=1) - 1
    slot = jnp.where(named, upto, -1)
    pack = (slot[:, None, :] == jnp.arange(cap, dtype=jnp.int32)[None, :, None]).astype(jnp.bfloat16)

    boxed = nodes == 2 and locals_ == 2 * SPLIT
    if boxed:
        gathered = gather_tokens(tokens, locals_ // 4).reshape(devices * rows, width)
    else:
        gathered = lax.all_gather(tokens, "local", axis=0, tiled=True)
        gathered = lax.all_gather(gathered, "node", axis=0, tiled=True)
    gate = jnp.dot(gathered, w_gate, preferred_element_type=jnp.float32)
    up = jnp.dot(gathered, w_up, preferred_element_type=jnp.float32)
    hidden = (jax.nn.silu(gate) * up * route_mine.reshape(-1, 1)).astype(jnp.bfloat16)
    packed = jnp.einsum("sct,sth->sch", pack, hidden.reshape(devices, rows, -1),
                        preferred_element_type=jnp.float32).astype(jnp.bfloat16)
    packed = packed.reshape(devices * cap, -1)
    if boxed:
        whole = gather_hidden(packed)
    else:
        groups = [list(range(h * SPLIT, (h + 1) * SPLIT)) for h in range(halves)]
        whole = lax.all_gather(packed, "local", axis=1, axis_index_groups=groups, tiled=True)
    out = jnp.dot(whole, w_down[0], preferred_element_type=jnp.float32).astype(jnp.bfloat16)
    out = jnp.einsum("sct,scd->std", pack, out.reshape(devices, cap, columns),
                     preferred_element_type=jnp.float32).astype(jnp.bfloat16)
    out = out.reshape(devices * rows, columns)
    half = lax.psum_scatter(out, "node", scatter_dimension=0, tiled=True)
    half = half.astype(jnp.bfloat16).reshape(locals_, rows, columns)
    back = lax.all_to_all(half, "local", split_axis=0, concat_axis=0, tiled=True)
    back = back.astype(jnp.float32).reshape(halves, SPLIT, rows, columns)
    mixed = jnp.sum(back, axis=0)
    return mixed.transpose(1, 0, 2).reshape(rows, width).astype(jnp.bfloat16)


def solution(mesh):
    placed = (
        P(("grp", "node", "local"), None),
        P(("grp", "node", "local"), None),
        P(("grp", "node", "local"), None),
        P(None, ("node", "local")),
        P(None, ("node", "local")),
        P(("node", "local"), None, None),
    )
    return jax.shard_map(
        on_device,
        mesh=mesh,
        in_specs=placed,
        out_specs=P(("grp", "node", "local"), None),
        check_vma=False,
    )
```

```python
import jax
import jax.numpy as jnp
from jax import lax
from jax.experimental import pallas as pl
from jax.experimental.pallas import tpu as pltpu
from jax.sharding import PartitionSpec as P

SPLIT = 8
MESH = pl.DeviceIdType.MESH


def device(core, local):
    return {"node": core, "local": local}


class Copies:
    def __init__(self, make, count):
        self.make = make
        self.count = count

    def start(self, at):
        self.make(at).start()

    def wait_send(self):
        for at in range(self.count):
            self.make(at).wait_send()


def token_gather(lines, own_ref, note_ref, all_ref, notes_ref, send_sem, recv_sem, own_sem):
    core, local = lax.axis_index("node"), lax.axis_index("local")
    count = lines * 4
    z, y, x = local // 4, local // 2 % 2, local % 2
    to_x, to_y = local + 1 - 2 * x, local + 2 - 4 * y
    first = (1 - core) * to_x + core * to_y
    second = core * to_x + (1 - core) * to_y
    below, above = local - 4, local + 4
    base, other = core * count, (1 - core) * count

    half = own_ref.shape[0] // 2
    place = pltpu.make_async_copy(own_ref, all_ref.at[base + local], own_sem.at[0])
    place.start()
    place_note = pltpu.make_async_copy(note_ref, notes_ref.at[base + local], own_sem.at[1])
    place_note.start()
    barrier = pltpu.get_barrier_semaphore()
    for peer in (device(core, first), device(core, second), device(1 - core, local)):
        pl.semaphore_signal(barrier, inc=1, device_id=peer, device_id_type=MESH)

    @pl.when(z > 0)
    def _():
        pl.semaphore_signal(barrier, inc=1, device_id=device(core, below), device_id_type=MESH)

    @pl.when(z < lines - 1)
    def _():
        pl.semaphore_signal(barrier, inc=1, device_id=device(core, above), device_id_type=MESH)

    ends = (z + lines - 2) // (lines - 1) + (2 * lines - 3 - z) // (lines - 1)
    pl.semaphore_wait(barrier, 3 + ends)
    place.wait()
    place_note.wait()

    def views(slot):
        return (
            all_ref.at[slot, pl.ds(0, half)],
            all_ref.at[slot, pl.ds(half, half)],
            notes_ref.at[slot],
        )

    def copy(source, kind, peer):
        def make(at):
            view = views(base + source)[at]
            return pltpu.make_async_remote_copy(
                src_ref=view,
                dst_ref=view,
                send_sem=send_sem.at[source, kind, at],
                recv_sem=recv_sem.at[base + source, at],
                device_id=peer,
                device_id_type=MESH,
            )

        return Copies(make, 3)

    def arrived(slot, at):
        view = views(slot)[at]
        pltpu.make_async_remote_copy(
            src_ref=view,
            dst_ref=view,
            send_sem=send_sem.at[0, 0, at],
            recv_sem=recv_sem.at[slot, at],
            device_id=device(1 - core, local),
            device_id_type=MESH,
        ).wait_recv()

    def up(source):
        return copy(source, 0, device(core, above))

    def down(source):
        return copy(source, 1, device(core, below))

    def to_second(source):
        return copy(source, 2, device(core, second))

    def to_first(source):
        return copy(source, 3, device(core, first))

    def to_core(source):
        return copy(source, 4, device(1 - core, local))

    def when(fits, action):
        @pl.when(fits)
        def _():
            action()

    def line(run):
        for step in range(lines):
            for sign in (-1, 1) if step else (0,):
                shift = sign * step
                fits = jnp.logical_and(z + shift >= 0, z + shift < lines)
                when(fits, lambda shift=shift, sign=sign: run(shift * 4, sign))

    def pass_on(shift, sign):
        source = local + shift
        for at in range(3):
            if sign:
                arrived(base + source, at)
            if sign <= 0:
                when(z < lines - 1, lambda: up(source).start(at))
            if sign >= 0:
                when(z > 0, lambda: down(source).start(at))
            to_second(source).start(at)
            to_first(source).start(at)
            to_core(source).start(at)

    def pass_first(shift, sign):
        source = first + shift
        for at in range(3):
            arrived(base + source, at)
            to_second(source).start(at)
            to_core(source).start(at)

    def pass_second(shift, sign, start):
        source = start + shift
        for at in range(3):
            arrived(base + source, at)
            to_core(source).start(at)

    opposite = first + second - local
    steps = []
    for step in range(lines):
        for sign in (-1, 1) if step else (0,):
            steps.append((step, sign))
    for at in range(len(steps) + 2):
        for lag, run in (
            (0, pass_on),
            (1, pass_first),
            (2, lambda a, b: (pass_second(a, b, second), pass_second(a, b, opposite))),
        ):
            if 0 <= at - lag < len(steps):
                step, sign = steps[at - lag]
                shift = step * sign
                fits = jnp.logical_and(z + shift >= 0, z + shift < lines)
                when(fits, lambda run=run, shift=shift, sign=sign: run(shift * 4, sign))
    for source in range(count):
        for at in range(3):
            arrived(other + source, at)

    def sent(shift, sign):
        source = local + shift
        if sign <= 0:
            when(z < lines - 1, lambda: up(source).wait_send())
        if sign >= 0:
            when(z > 0, lambda: down(source).wait_send())
        to_first(source).wait_send()
        to_second(source).wait_send()
        to_second(first + shift).wait_send()

    line(sent)
    for source in range(count):
        to_core(source).wait_send()


def hidden_gather(own_ref, all_ref, send_sem, recv_sem, own_sem):
    core, local = lax.axis_index("node"), lax.axis_index("local")
    rows, width = own_ref.shape
    third = -(-rows // 48) * 16
    cuts = [(0, third), (third, third), (2 * third, rows - 2 * third)]
    within = local % SPLIT
    flips = [(1 - 2 * (local // stride % 2)) * stride for stride in (1, 2, 4)]

    def block(index):
        return pl.ds(pl.multiple_of(index * width, width), width)

    place = pltpu.make_async_copy(own_ref, all_ref.at[:, block(within)], own_sem)
    place.start()
    barrier = pltpu.get_barrier_semaphore()
    for flip in flips:
        pl.semaphore_signal(barrier, inc=1, device_id=device(core, local + flip), device_id_type=MESH)
    pl.semaphore_wait(barrier, len(flips))
    place.wait()

    def copy(part, source, axis, peer):
        start, size = cuts[part]
        here = all_ref.at[pl.ds(start, size), block(source)]
        return pltpu.make_async_remote_copy(
            src_ref=here,
            dst_ref=here,
            send_sem=send_sem.at[part, axis, source],
            recv_sem=recv_sem.at[part, source],
            device_id=device(core, peer),
            device_id_type=MESH,
        )

    pending = []

    def send(part, source, axes):
        for axis in axes:
            moved = copy(part, source, axis, local + flips[axis])
            moved.start()
            pending.append(moved)

    orders = [[(part + turn) % 3 for turn in range(3)] for part in range(3)]
    held = [[within] for _ in range(3)]
    for part, order in enumerate(orders):
        send(part, within, order)
    for turn in range(3):
        for place_in in range(2**turn):
            for part, order in enumerate(orders):
                source = held[part][place_in] + flips[order[turn]]
                copy(part, source, 0, local + flips[order[turn]]).wait_recv()
                send(part, source, order[turn + 1 :])
                held[part].append(source)
    for moved in pending:
        moved.wait_send()


def gather_tokens(tokens, note, lines):
    rows, width = tokens.shape
    count = lines * 4
    return pl.pallas_call(
        lambda *refs: token_gather(lines, *refs),
        out_shape=(
            jax.ShapeDtypeStruct((2 * count, rows, width), tokens.dtype),
            jax.ShapeDtypeStruct((2 * count,) + note.shape, note.dtype),
        ),
        in_specs=[pl.BlockSpec(memory_space=pl.ANY)] * 2,
        out_specs=(pl.BlockSpec(memory_space=pl.ANY),) * 2,
        scratch_shapes=[
            pltpu.SemaphoreType.DMA((count, 5, 3)),
            pltpu.SemaphoreType.DMA((2 * count, 3)),
            pltpu.SemaphoreType.DMA((2,)),
        ],
        compiler_params=pltpu.CompilerParams(collective_id=0, has_side_effects=True),
    )(tokens, note)


def gather_hidden(packed):
    rows, width = packed.shape
    return pl.pallas_call(
        hidden_gather,
        out_shape=jax.ShapeDtypeStruct((rows, SPLIT * width), packed.dtype),
        in_specs=[pl.BlockSpec(memory_space=pl.ANY)],
        out_specs=pl.BlockSpec(memory_space=pl.ANY),
        scratch_shapes=[
            pltpu.SemaphoreType.DMA((3, 3, SPLIT)),
            pltpu.SemaphoreType.DMA((3, SPLIT)),
            pltpu.SemaphoreType.DMA,
        ],
        compiler_params=pltpu.CompilerParams(collective_id=1, has_side_effects=True),
    )(packed)


def on_device(tokens, expert_ids, scores, w_gate, w_up, w_down):
    rows, width = tokens.shape
    nodes, locals_ = lax.axis_size("node"), lax.axis_size("local")
    devices = nodes * locals_
    experts = devices // SPLIT
    halves = locals_ // SPLIT
    top = expert_ids.shape[1]
    cap = min(rows, max(2, rows * top * 5 // (experts * 4)))
    columns = w_down.shape[2]
    mine = lax.axis_index("node") * halves + lax.axis_index("local") // SPLIT

    weights = 2.5 * scores / jnp.sum(scores, axis=1, keepdims=True)
    hot = expert_ids[:, :, None] == jnp.arange(experts, dtype=jnp.int32)
    route = jnp.sum(jnp.where(hot, weights[:, :, None], 0.0), axis=1)
    route = route.astype(jnp.bfloat16)
    boxed = nodes == 2 and locals_ == 2 * SPLIT and experts <= 16 and rows <= 128 and rows % 32 == 0
    if boxed:
        note = jnp.pad(route.T, ((0, 16 - experts), (0, 128 - rows)))
        gathered, notes = gather_tokens(tokens, note, locals_ // 4)
        gathered = gathered.reshape(devices * rows, width)
        route = notes[:, :experts, :rows].transpose(0, 2, 1)
    else:
        gathered = lax.all_gather(tokens, "local", axis=0, tiled=True)
        gathered = lax.all_gather(gathered, "node", axis=0, tiled=True)
        route = lax.all_gather(route, ("node", "local"), axis=0)
    route_mine = lax.dynamic_slice_in_dim(route, mine, 1, 2)[:, :, 0].astype(jnp.float32)
    named = route_mine > 0
    upto = jnp.cumsum(named.astype(jnp.int32), axis=1) - 1
    slot = jnp.where(named, upto, -1)
    pack = (slot[:, None, :] == jnp.arange(cap, dtype=jnp.int32)[None, :, None]).astype(jnp.bfloat16)

    gate = jnp.dot(gathered, w_gate, preferred_element_type=jnp.float32)
    up = jnp.dot(gathered, w_up, preferred_element_type=jnp.float32)
    hidden = (jax.nn.silu(gate) * up * route_mine.reshape(-1, 1)).astype(jnp.bfloat16)
    packed = jnp.einsum("sct,sth->sch", pack, hidden.reshape(devices, rows, -1),
                        preferred_element_type=jnp.float32).astype(jnp.bfloat16)
    packed = packed.reshape(devices * cap, -1)
    if boxed:
        whole = gather_hidden(packed)
    else:
        groups = [list(range(h * SPLIT, (h + 1) * SPLIT)) for h in range(halves)]
        whole = lax.all_gather(packed, "local", axis=1, axis_index_groups=groups, tiled=True)
    out = jnp.dot(whole, w_down[0], preferred_element_type=jnp.float32).astype(jnp.bfloat16)
    out = jnp.einsum("sct,scd->std", pack, out.reshape(devices, cap, columns),
                     preferred_element_type=jnp.float32).astype(jnp.bfloat16)
    out = out.reshape(devices * rows, columns)
    half = lax.psum_scatter(out, "node", scatter_dimension=0, tiled=True)
    half = half.astype(jnp.bfloat16).reshape(locals_, rows, columns)
    back = lax.all_to_all(half, "local", split_axis=0, concat_axis=0, tiled=True)
    back = back.astype(jnp.float32).reshape(halves, SPLIT, rows, columns)
    mixed = jnp.sum(back, axis=0)
    return mixed.transpose(1, 0, 2).reshape(rows, width).astype(jnp.bfloat16)


def solution(mesh):
    placed = (
        P(("grp", "node", "local"), None),
        P(("grp", "node", "local"), None),
        P(("grp", "node", "local"), None),
        P(None, ("node", "local")),
        P(None, ("node", "local")),
        P(("node", "local"), None, None),
    )
    return jax.shard_map(
        on_device,
        mesh=mesh,
        in_specs=placed,
        out_specs=P(("grp", "node", "local"), None),
        check_vma=False,
    )
```

```python
import jax
import jax.numpy as jnp
from jax import lax
from jax.experimental import pallas as pl
from jax.experimental.pallas import tpu as pltpu
from jax.sharding import PartitionSpec as P

SPLIT = 8
MESH = pl.DeviceIdType.MESH


def device(core, local):
    return {"node": core, "local": local}


class Copies:
    def __init__(self, make):
        self.make = make

    def start(self, at):
        self.make(at).start()

    def wait_send(self, pieces):
        for at in pieces:
            self.make(at).wait_send()


def token_gather(lines, own_ref, note_ref, all_ref, notes_ref, send_sem, recv_sem, own_sem):
    core, local = lax.axis_index("node"), lax.axis_index("local")
    count = lines * 4
    z, y, x = local // 4, local // 2 % 2, local % 2
    to_x, to_y = local + 1 - 2 * x, local + 2 - 4 * y
    first = (1 - core) * to_x + core * to_y
    second = core * to_x + (1 - core) * to_y
    below, above = local - 4, local + 4
    base, other = core * count, (1 - core) * count

    quarter = own_ref.shape[0] // 4
    place = pltpu.make_async_copy(own_ref, all_ref.at[base + local], own_sem.at[0])
    place.start()
    place_note = pltpu.make_async_copy(note_ref, notes_ref.at[base + local], own_sem.at[1])
    place_note.start()
    barrier = pltpu.get_barrier_semaphore()
    for peer in (device(core, first), device(core, second), device(1 - core, local)):
        pl.semaphore_signal(barrier, inc=1, device_id=peer, device_id_type=MESH)

    @pl.when(z > 0)
    def _():
        pl.semaphore_signal(barrier, inc=1, device_id=device(core, below), device_id_type=MESH)

    @pl.when(z < lines - 1)
    def _():
        pl.semaphore_signal(barrier, inc=1, device_id=device(core, above), device_id_type=MESH)

    ends = (z + lines - 2) // (lines - 1) + (2 * lines - 3 - z) // (lines - 1)
    pl.semaphore_wait(barrier, 3 + ends)
    place.wait()
    place_note.wait()

    def views(slot):
        return (
            all_ref.at[slot, pl.ds(0, 2 * quarter)],
            all_ref.at[slot, pl.ds(2 * quarter, quarter)],
            notes_ref.at[slot],
            all_ref.at[slot, pl.ds(3 * quarter, quarter)],
        )

    def copy(source, kind, peer):
        def make(at):
            view = views(base + source)[at]
            return pltpu.make_async_remote_copy(
                src_ref=view,
                dst_ref=view,
                send_sem=send_sem.at[source, kind, at],
                recv_sem=recv_sem.at[base + source, at],
                device_id=peer,
                device_id_type=MESH,
            )

        return Copies(make)

    def arrived(slot, at):
        view = views(slot)[at]
        pltpu.make_async_remote_copy(
            src_ref=view,
            dst_ref=view,
            send_sem=send_sem.at[0, 0, at],
            recv_sem=recv_sem.at[slot, at],
            device_id=device(1 - core, local),
            device_id_type=MESH,
        ).wait_recv()

    def up(source):
        return copy(source, 0, device(core, above))

    def down(source):
        return copy(source, 1, device(core, below))

    def to_second(source):
        return copy(source, 2, device(core, second))

    def to_first(source):
        return copy(source, 3, device(core, first))

    def to_core(source):
        return copy(source, 4, device(1 - core, local))

    def when(fits, action):
        @pl.when(fits)
        def _():
            action()

    def line(run):
        for step in range(lines):
            for sign in (-1, 1) if step else (0,):
                shift = sign * step
                fits = jnp.logical_and(z + shift >= 0, z + shift < lines)
                when(fits, lambda shift=shift, sign=sign: run(shift * 4, sign))

    def pass_on(shift, sign):
        source = local + shift
        for at in range(3):
            if sign:
                arrived(base + source, at)
            if sign <= 0:
                when(z < lines - 1, lambda: up(source).start(at))
            if sign >= 0:
                when(z > 0, lambda: down(source).start(at))
            to_second(source).start(at)
            to_first(source).start(at)
            to_core(source).start(at)

    def pass_first(shift, sign):
        source = first + shift
        for at in range(3):
            arrived(base + source, at)
            to_second(source).start(at)
            to_core(source).start(at)

    def pass_second(shift, sign, start):
        source = start + shift
        for at in range(3):
            arrived(base + source, at)
            to_core(source).start(at)

    opposite = first + second - local
    plane = (local, first, second, opposite)

    def plane_step(at):
        for source in ((local,), (first,), (second, opposite))[at]:
            if at:
                arrived(base + source, 3)
            if at == 0:
                to_first(source).start(3)
            if at <= 1:
                to_second(source).start(3)
            when(z < lines - 1, lambda source=source: up(source).start(3))
            when(z > 0, lambda source=source: down(source).start(3))
            to_core(source).start(3)

    def along(shift, sign):
        for start in plane:
            source = start + shift
            arrived(base + source, 3)
            if sign < 0:
                when(z < lines - 1, lambda source=source: up(source).start(3))
            else:
                when(z > 0, lambda source=source: down(source).start(3))
            to_core(source).start(3)

    steps = []
    for step in range(lines):
        for sign in (-1, 1) if step else (0,):
            steps.append((step, sign))
    for at in range(len(steps) + 2):
        for lag, run in (
            (0, pass_on),
            (1, pass_first),
            (2, lambda a, b: (pass_second(a, b, second), pass_second(a, b, opposite))),
        ):
            if 0 <= at - lag < len(steps):
                step, sign = steps[at - lag]
                shift = step * sign
                fits = jnp.logical_and(z + shift >= 0, z + shift < lines)
                when(fits, lambda run=run, shift=shift, sign=sign: run(shift * 4, sign))
        if at < 3:
            plane_step(at)
        elif at - 2 < len(steps):
            step, sign = steps[at - 2]
            shift = step * sign
            fits = jnp.logical_and(z + shift >= 0, z + shift < lines)
            when(fits, lambda shift=shift, sign=sign: along(shift * 4, sign))
    for source in range(count):
        for at in range(4):
            arrived(other + source, at)

    def sent(shift, sign):
        source = local + shift
        if sign <= 0:
            when(z < lines - 1, lambda: up(source).wait_send(range(4)))
        if sign >= 0:
            when(z > 0, lambda: down(source).wait_send(range(4)))
        to_first(source).wait_send(range(3))
        to_second(source).wait_send(range(3))
        to_second(first + shift).wait_send(range(3))
        for start in plane[1:]:
            if sign <= 0:
                when(z < lines - 1, lambda start=start: up(start + shift).wait_send([3]))
            if sign >= 0:
                when(z > 0, lambda start=start: down(start + shift).wait_send([3]))

    line(sent)
    to_first(local).wait_send([3])
    to_second(local).wait_send([3])
    to_second(first).wait_send([3])
    for source in range(count):
        to_core(source).wait_send(range(4))


def hidden_gather(own_ref, all_ref, send_sem, recv_sem, own_sem):
    core, local = lax.axis_index("node"), lax.axis_index("local")
    rows, width = own_ref.shape
    third = -(-rows // 48) * 16
    cuts = [(0, third), (third, third), (2 * third, rows - 2 * third)]
    within = local % SPLIT
    flips = [(1 - 2 * (local // stride % 2)) * stride for stride in (1, 2, 4)]

    def block(index):
        return pl.ds(pl.multiple_of(index * width, width), width)

    place = pltpu.make_async_copy(own_ref, all_ref.at[:, block(within)], own_sem)
    place.start()
    barrier = pltpu.get_barrier_semaphore()
    for flip in flips:
        pl.semaphore_signal(barrier, inc=1, device_id=device(core, local + flip), device_id_type=MESH)
    pl.semaphore_wait(barrier, len(flips))
    place.wait()

    def copy(part, source, axis, peer):
        start, size = cuts[part]
        here = all_ref.at[pl.ds(start, size), block(source)]
        return pltpu.make_async_remote_copy(
            src_ref=here,
            dst_ref=here,
            send_sem=send_sem.at[part, axis, source],
            recv_sem=recv_sem.at[part, source],
            device_id=device(core, peer),
            device_id_type=MESH,
        )

    pending = []

    def send(part, source, axes):
        for axis in axes:
            moved = copy(part, source, axis, local + flips[axis])
            moved.start()
            pending.append(moved)

    orders = [[(part + turn) % 3 for turn in range(3)] for part in range(3)]
    held = [[within] for _ in range(3)]
    for part, order in enumerate(orders):
        send(part, within, order)
    for turn in range(3):
        for place_in in range(2**turn):
            for part, order in enumerate(orders):
                source = held[part][place_in] + flips[order[turn]]
                copy(part, source, 0, local + flips[order[turn]]).wait_recv()
                send(part, source, order[turn + 1 :])
                held[part].append(source)
    for moved in pending:
        moved.wait_send()


def gather_tokens(tokens, note, lines):
    rows, width = tokens.shape
    count = lines * 4
    return pl.pallas_call(
        lambda *refs: token_gather(lines, *refs),
        out_shape=(
            jax.ShapeDtypeStruct((2 * count, rows, width), tokens.dtype),
            jax.ShapeDtypeStruct((2 * count,) + note.shape, note.dtype),
        ),
        in_specs=[pl.BlockSpec(memory_space=pl.ANY)] * 2,
        out_specs=(pl.BlockSpec(memory_space=pl.ANY),) * 2,
        scratch_shapes=[
            pltpu.SemaphoreType.DMA((count, 5, 4)),
            pltpu.SemaphoreType.DMA((2 * count, 4)),
            pltpu.SemaphoreType.DMA((2,)),
        ],
        compiler_params=pltpu.CompilerParams(collective_id=0, has_side_effects=True),
    )(tokens, note)


def gated(rows_ref, scale_ref, gate_ref, up_ref, out_ref):
    gate = jnp.dot(rows_ref[...], gate_ref[...], preferred_element_type=jnp.float32)
    up = jnp.dot(rows_ref[...], up_ref[...], preferred_element_type=jnp.float32)
    out_ref[...] = (gate / (1.0 + jnp.exp(-gate)) * up * scale_ref[...]).astype(out_ref.dtype)


def expert_hidden(gathered, scale, w_gate, w_up):
    total, width = gathered.shape
    units = w_gate.shape[1]
    tile = 256
    return pl.pallas_call(
        gated,
        out_shape=jax.ShapeDtypeStruct((total, units), jnp.bfloat16),
        grid=(total // tile,),
        in_specs=[
            pl.BlockSpec((tile, width), lambda i: (i, 0)),
            pl.BlockSpec((tile, 1), lambda i: (i, 0)),
            pl.BlockSpec((width, units), lambda i: (0, 0)),
            pl.BlockSpec((width, units), lambda i: (0, 0)),
        ],
        out_specs=pl.BlockSpec((tile, units), lambda i: (i, 0)),
        compiler_params=pltpu.CompilerParams(vmem_limit_bytes=40 * 2**20),
        cost_estimate=pl.CostEstimate(
            flops=4 * total * width * units, bytes_accessed=2 * total * width, transcendentals=total * units
        ),
    )(gathered, scale, w_gate, w_up)


def gather_hidden(packed):
    rows, width = packed.shape
    return pl.pallas_call(
        hidden_gather,
        out_shape=jax.ShapeDtypeStruct((rows, SPLIT * width), packed.dtype),
        in_specs=[pl.BlockSpec(memory_space=pl.ANY)],
        out_specs=pl.BlockSpec(memory_space=pl.ANY),
        scratch_shapes=[
            pltpu.SemaphoreType.DMA((3, 3, SPLIT)),
            pltpu.SemaphoreType.DMA((3, SPLIT)),
            pltpu.SemaphoreType.DMA,
        ],
        compiler_params=pltpu.CompilerParams(collective_id=1, has_side_effects=True),
    )(packed)


def on_device(tokens, expert_ids, scores, w_gate, w_up, w_down):
    rows, width = tokens.shape
    nodes, locals_ = lax.axis_size("node"), lax.axis_size("local")
    devices = nodes * locals_
    experts = devices // SPLIT
    halves = locals_ // SPLIT
    top = expert_ids.shape[1]
    cap = min(rows, max(2, rows * top * 5 // (experts * 4)))
    columns = w_down.shape[2]
    mine = lax.axis_index("node") * halves + lax.axis_index("local") // SPLIT

    weights = 2.5 * scores / jnp.sum(scores, axis=1, keepdims=True)
    hot = expert_ids[:, :, None] == jnp.arange(experts, dtype=jnp.int32)
    route = jnp.sum(jnp.where(hot, weights[:, :, None], 0.0), axis=1)
    route = route.astype(jnp.bfloat16)
    boxed = nodes == 2 and locals_ == 2 * SPLIT and experts <= 16 and rows <= 128 and rows % 64 == 0
    if boxed:
        note = jnp.pad(route.T, ((0, 16 - experts), (0, 128 - rows)))
        gathered, notes = gather_tokens(tokens, note, locals_ // 4)
        gathered = gathered.reshape(devices * rows, width)
        route = notes[:, :experts, :rows].transpose(0, 2, 1)
    else:
        gathered = lax.all_gather(tokens, "local", axis=0, tiled=True)
        gathered = lax.all_gather(gathered, "node", axis=0, tiled=True)
        route = lax.all_gather(route, ("node", "local"), axis=0)
    route_mine = lax.dynamic_slice_in_dim(route, mine, 1, 2)[:, :, 0].astype(jnp.float32)
    named = route_mine > 0
    upto = jnp.cumsum(named.astype(jnp.int32), axis=1) - 1
    slot = jnp.where(named, upto, -1)
    pack = (slot[:, None, :] == jnp.arange(cap, dtype=jnp.int32)[None, :, None]).astype(jnp.bfloat16)

    hidden = expert_hidden(gathered, route_mine.reshape(-1, 1), w_gate, w_up)
    packed = jnp.einsum("sct,sth->sch", pack, hidden.reshape(devices, rows, -1),
                        preferred_element_type=jnp.float32).astype(jnp.bfloat16)
    packed = packed.reshape(devices * cap, -1)
    if boxed:
        whole = gather_hidden(packed)
    else:
        groups = [list(range(h * SPLIT, (h + 1) * SPLIT)) for h in range(halves)]
        whole = lax.all_gather(packed, "local", axis=1, axis_index_groups=groups, tiled=True)
    out = jnp.dot(whole, w_down[0], preferred_element_type=jnp.float32).astype(jnp.bfloat16)
    out = jnp.einsum("sct,scd->std", pack, out.reshape(devices, cap, columns),
                     preferred_element_type=jnp.float32).astype(jnp.bfloat16)
    out = out.reshape(devices * rows, columns)
    half = lax.psum_scatter(out, "node", scatter_dimension=0, tiled=True)
    half = half.astype(jnp.bfloat16).reshape(locals_, rows, columns)
    back = lax.all_to_all(half, "local", split_axis=0, concat_axis=0, tiled=True)
    back = back.astype(jnp.float32).reshape(halves, SPLIT, rows, columns)
    mixed = jnp.sum(back, axis=0)
    return mixed.transpose(1, 0, 2).reshape(rows, width).astype(jnp.bfloat16)


def solution(mesh):
    placed = (
        P(("grp", "node", "local"), None),
        P(("grp", "node", "local"), None),
        P(("grp", "node", "local"), None),
        P(None, ("node", "local")),
        P(None, ("node", "local")),
        P(("node", "local"), None, None),
    )
    return jax.shard_map(
        on_device,
        mesh=mesh,
        in_specs=placed,
        out_specs=P(("grp", "node", "local"), None),
        check_vma=False,
    )
```

```python
import jax
import jax.numpy as jnp
from jax import lax
from jax.experimental import pallas as pl
from jax.experimental.pallas import tpu as pltpu
from jax.sharding import PartitionSpec as P

SPLIT = 8
MESH = pl.DeviceIdType.MESH


def device(core, local):
    return {"node": core, "local": local}


class Copies:
    def __init__(self, make):
        self.make = make

    def start(self, at):
        self.make(at).start()

    def wait_send(self, pieces):
        for at in pieces:
            self.make(at).wait_send()


def token_gather(lines, own_ref, note_ref, all_ref, notes_ref, send_sem, recv_sem, own_sem):
    core, local = lax.axis_index("node"), lax.axis_index("local")
    count = lines * 4
    z, y, x = local // 4, local // 2 % 2, local % 2
    to_x, to_y = local + 1 - 2 * x, local + 2 - 4 * y
    first = (1 - core) * to_x + core * to_y
    second = core * to_x + (1 - core) * to_y
    below, above = local - 4, local + 4
    base, other = core * count, (1 - core) * count

    quarter = own_ref.shape[0] // 4
    place = pltpu.make_async_copy(own_ref, all_ref.at[base + local], own_sem.at[0])
    place.start()
    place_note = pltpu.make_async_copy(note_ref, notes_ref.at[base + local], own_sem.at[1])
    place_note.start()
    barrier = pltpu.get_barrier_semaphore()
    for peer in (device(core, first), device(core, second), device(1 - core, local)):
        pl.semaphore_signal(barrier, inc=1, device_id=peer, device_id_type=MESH)

    @pl.when(z > 0)
    def _():
        pl.semaphore_signal(barrier, inc=1, device_id=device(core, below), device_id_type=MESH)

    @pl.when(z < lines - 1)
    def _():
        pl.semaphore_signal(barrier, inc=1, device_id=device(core, above), device_id_type=MESH)

    ends = (z + lines - 2) // (lines - 1) + (2 * lines - 3 - z) // (lines - 1)
    pl.semaphore_wait(barrier, 3 + ends)
    place.wait()
    place_note.wait()

    def views(slot):
        return (
            all_ref.at[slot, pl.ds(0, 2 * quarter)],
            all_ref.at[slot, pl.ds(2 * quarter, quarter)],
            notes_ref.at[slot],
            all_ref.at[slot, pl.ds(3 * quarter, quarter)],
        )

    def copy(source, kind, peer):
        def make(at):
            view = views(base + source)[at]
            return pltpu.make_async_remote_copy(
                src_ref=view,
                dst_ref=view,
                send_sem=send_sem.at[source, kind, at],
                recv_sem=recv_sem.at[base + source, at],
                device_id=peer,
                device_id_type=MESH,
            )

        return Copies(make)

    def arrived(slot, at):
        view = views(slot)[at]
        pltpu.make_async_remote_copy(
            src_ref=view,
            dst_ref=view,
            send_sem=send_sem.at[0, 0, at],
            recv_sem=recv_sem.at[slot, at],
            device_id=device(1 - core, local),
            device_id_type=MESH,
        ).wait_recv()

    def up(source):
        return copy(source, 0, device(core, above))

    def down(source):
        return copy(source, 1, device(core, below))

    def to_second(source):
        return copy(source, 2, device(core, second))

    def to_first(source):
        return copy(source, 3, device(core, first))

    def to_core(source):
        return copy(source, 4, device(1 - core, local))

    def when(fits, action):
        @pl.when(fits)
        def _():
            action()

    def line(run):
        for step in range(lines):
            for sign in (-1, 1) if step else (0,):
                shift = sign * step
                fits = jnp.logical_and(z + shift >= 0, z + shift < lines)
                when(fits, lambda shift=shift, sign=sign: run(shift * 4, sign))

    def pass_on(shift, sign):
        source = local + shift
        for at in range(3):
            if sign:
                arrived(base + source, at)
            if sign <= 0:
                when(z < lines - 1, lambda: up(source).start(at))
            if sign >= 0:
                when(z > 0, lambda: down(source).start(at))
            to_second(source).start(at)
            to_first(source).start(at)
            to_core(source).start(at)

    def pass_first(shift, sign):
        source = first + shift
        for at in range(3):
            arrived(base + source, at)
            to_second(source).start(at)
            to_core(source).start(at)

    def pass_second(shift, sign, start):
        source = start + shift
        for at in range(3):
            arrived(base + source, at)
            to_core(source).start(at)

    opposite = first + second - local
    plane = (local, first, second, opposite)

    def plane_step(at):
        for source in ((local,), (first,), (second, opposite))[at]:
            if at:
                arrived(base + source, 3)
            if at == 0:
                to_first(source).start(3)
            if at <= 1:
                to_second(source).start(3)
            when(z < lines - 1, lambda source=source: up(source).start(3))
            when(z > 0, lambda source=source: down(source).start(3))
            to_core(source).start(3)

    def along(shift, sign):
        for start in plane:
            source = start + shift
            arrived(base + source, 3)
            if sign < 0:
                when(z < lines - 1, lambda source=source: up(source).start(3))
            else:
                when(z > 0, lambda source=source: down(source).start(3))
            to_core(source).start(3)

    steps = []
    for step in range(lines):
        for sign in (-1, 1) if step else (0,):
            steps.append((step, sign))
    for at in range(len(steps) + 2):
        for lag, run in (
            (0, pass_on),
            (1, pass_first),
            (2, lambda a, b: (pass_second(a, b, second), pass_second(a, b, opposite))),
        ):
            if 0 <= at - lag < len(steps):
                step, sign = steps[at - lag]
                shift = step * sign
                fits = jnp.logical_and(z + shift >= 0, z + shift < lines)
                when(fits, lambda run=run, shift=shift, sign=sign: run(shift * 4, sign))
        if at < 3:
            plane_step(at)
        elif at - 2 < len(steps):
            step, sign = steps[at - 2]
            shift = step * sign
            fits = jnp.logical_and(z + shift >= 0, z + shift < lines)
            when(fits, lambda shift=shift, sign=sign: along(shift * 4, sign))
    for source in range(count):
        for at in range(4):
            arrived(other + source, at)

    def sent(shift, sign):
        source = local + shift
        if sign <= 0:
            when(z < lines - 1, lambda: up(source).wait_send(range(4)))
        if sign >= 0:
            when(z > 0, lambda: down(source).wait_send(range(4)))
        to_first(source).wait_send(range(3))
        to_second(source).wait_send(range(3))
        to_second(first + shift).wait_send(range(3))
        for start in plane[1:]:
            if sign <= 0:
                when(z < lines - 1, lambda start=start: up(start + shift).wait_send([3]))
            if sign >= 0:
                when(z > 0, lambda start=start: down(start + shift).wait_send([3]))

    line(sent)
    to_first(local).wait_send([3])
    to_second(local).wait_send([3])
    to_second(first).wait_send([3])
    for source in range(count):
        to_core(source).wait_send(range(4))


def hidden_gather(own_ref, all_ref, send_sem, recv_sem, own_sem):
    core, local = lax.axis_index("node"), lax.axis_index("local")
    rows, width = own_ref.shape
    third = -(-rows // 48) * 16
    cuts = [(0, third), (third, third), (2 * third, rows - 2 * third)]
    within = local % SPLIT
    flips = [(1 - 2 * (local // stride % 2)) * stride for stride in (1, 2, 4)]

    place = pltpu.make_async_copy(own_ref, all_ref.at[within], own_sem)
    place.start()
    barrier = pltpu.get_barrier_semaphore()
    for flip in flips:
        pl.semaphore_signal(barrier, inc=1, device_id=device(core, local + flip), device_id_type=MESH)
    pl.semaphore_wait(barrier, len(flips))
    place.wait()

    def copy(part, source, axis, peer):
        start, size = cuts[part]
        here = all_ref.at[source, pl.ds(start, size)]
        return pltpu.make_async_remote_copy(
            src_ref=here,
            dst_ref=here,
            send_sem=send_sem.at[part, axis, source],
            recv_sem=recv_sem.at[part, source],
            device_id=device(core, peer),
            device_id_type=MESH,
        )

    pending = []

    def send(part, source, axes):
        for axis in axes:
            moved = copy(part, source, axis, local + flips[axis])
            moved.start()
            pending.append(moved)

    orders = [[(part + turn) % 3 for turn in range(3)] for part in range(3)]
    held = [[within] for _ in range(3)]
    for part, order in enumerate(orders):
        send(part, within, order)
    for turn in range(3):
        for place_in in range(2**turn):
            for part, order in enumerate(orders):
                source = held[part][place_in] + flips[order[turn]]
                copy(part, source, 0, local + flips[order[turn]]).wait_recv()
                send(part, source, order[turn + 1 :])
                held[part].append(source)
    for moved in pending:
        moved.wait_send()


def down(parts_ref, weight_ref, out_ref):
    parts, _, width = parts_ref.shape
    rows = jnp.concatenate([parts_ref[part] for part in range(parts)], axis=1)
    out_ref[...] = jnp.dot(rows, weight_ref[...], preferred_element_type=jnp.float32).astype(out_ref.dtype)


def expert_out(parts, weight):
    count, total, width = parts.shape
    columns = weight.shape[1]
    tile = 256
    return pl.pallas_call(
        down,
        out_shape=jax.ShapeDtypeStruct((total, columns), jnp.bfloat16),
        grid=(pl.cdiv(total, tile),),
        in_specs=[
            pl.BlockSpec((count, tile, width), lambda i: (0, i, 0)),
            pl.BlockSpec((count * width, columns), lambda i: (0, 0)),
        ],
        out_specs=pl.BlockSpec((tile, columns), lambda i: (i, 0)),
        compiler_params=pltpu.CompilerParams(vmem_limit_bytes=32 * 2**20),
        cost_estimate=pl.CostEstimate(
            flops=2 * total * count * width * columns, bytes_accessed=4 * total * columns, transcendentals=0
        ),
    )(parts, weight)


def gather_tokens(tokens, note, lines):
    rows, width = tokens.shape
    count = lines * 4
    return pl.pallas_call(
        lambda *refs: token_gather(lines, *refs),
        out_shape=(
            jax.ShapeDtypeStruct((2 * count, rows, width), tokens.dtype),
            jax.ShapeDtypeStruct((2 * count,) + note.shape, note.dtype),
        ),
        in_specs=[pl.BlockSpec(memory_space=pl.ANY)] * 2,
        out_specs=(pl.BlockSpec(memory_space=pl.ANY),) * 2,
        scratch_shapes=[
            pltpu.SemaphoreType.DMA((count, 5, 4)),
            pltpu.SemaphoreType.DMA((2 * count, 4)),
            pltpu.SemaphoreType.DMA((2,)),
        ],
        compiler_params=pltpu.CompilerParams(collective_id=0, has_side_effects=True),
    )(tokens, note)


def gated(rows_ref, scale_ref, gate_ref, up_ref, out_ref):
    gate = jnp.dot(rows_ref[...], gate_ref[...], preferred_element_type=jnp.float32)
    up = jnp.dot(rows_ref[...], up_ref[...], preferred_element_type=jnp.float32)
    out_ref[...] = (gate / (1.0 + jnp.exp(-gate)) * up * scale_ref[...]).astype(out_ref.dtype)


def expert_hidden(gathered, scale, w_gate, w_up):
    total, width = gathered.shape
    units = w_gate.shape[1]
    tile = 256
    return pl.pallas_call(
        gated,
        out_shape=jax.ShapeDtypeStruct((total, units), jnp.bfloat16),
        grid=(total // tile,),
        in_specs=[
            pl.BlockSpec((tile, width), lambda i: (i, 0)),
            pl.BlockSpec((tile, 1), lambda i: (i, 0)),
            pl.BlockSpec((width, units), lambda i: (0, 0)),
            pl.BlockSpec((width, units), lambda i: (0, 0)),
        ],
        out_specs=pl.BlockSpec((tile, units), lambda i: (i, 0)),
        compiler_params=pltpu.CompilerParams(vmem_limit_bytes=40 * 2**20),
        cost_estimate=pl.CostEstimate(
            flops=4 * total * width * units, bytes_accessed=2 * total * width, transcendentals=total * units
        ),
    )(gathered, scale, w_gate, w_up)


def gather_hidden(packed):
    rows, width = packed.shape
    return pl.pallas_call(
        hidden_gather,
        out_shape=jax.ShapeDtypeStruct((SPLIT, rows, width), packed.dtype),
        in_specs=[pl.BlockSpec(memory_space=pl.ANY)],
        out_specs=pl.BlockSpec(memory_space=pl.ANY),
        scratch_shapes=[
            pltpu.SemaphoreType.DMA((3, 3, SPLIT)),
            pltpu.SemaphoreType.DMA((3, SPLIT)),
            pltpu.SemaphoreType.DMA,
        ],
        compiler_params=pltpu.CompilerParams(collective_id=1, has_side_effects=True),
    )(packed)


def on_device(tokens, expert_ids, scores, w_gate, w_up, w_down):
    rows, width = tokens.shape
    nodes, locals_ = lax.axis_size("node"), lax.axis_size("local")
    devices = nodes * locals_
    experts = devices // SPLIT
    halves = locals_ // SPLIT
    top = expert_ids.shape[1]
    cap = min(rows, max(2, rows * top * 5 // (experts * 4)))
    columns = w_down.shape[2]
    mine = lax.axis_index("node") * halves + lax.axis_index("local") // SPLIT

    weights = 2.5 * scores / jnp.sum(scores, axis=1, keepdims=True)
    hot = expert_ids[:, :, None] == jnp.arange(experts, dtype=jnp.int32)
    route = jnp.sum(jnp.where(hot, weights[:, :, None], 0.0), axis=1)
    route = route.astype(jnp.bfloat16)
    boxed = nodes == 2 and locals_ == 2 * SPLIT and experts <= 16 and rows <= 128 and rows % 64 == 0
    if boxed:
        note = jnp.pad(route.T, ((0, 16 - experts), (0, 128 - rows)))
        gathered, notes = gather_tokens(tokens, note, locals_ // 4)
        gathered = gathered.reshape(devices * rows, width)
        route = notes[:, :experts, :rows].transpose(0, 2, 1)
    else:
        gathered = lax.all_gather(tokens, "local", axis=0, tiled=True)
        gathered = lax.all_gather(gathered, "node", axis=0, tiled=True)
        route = lax.all_gather(route, ("node", "local"), axis=0)
    route_mine = lax.dynamic_slice_in_dim(route, mine, 1, 2)[:, :, 0].astype(jnp.float32)
    named = route_mine > 0
    upto = jnp.cumsum(named.astype(jnp.int32), axis=1) - 1
    slot = jnp.where(named, upto, -1)
    pack = (slot[:, None, :] == jnp.arange(cap, dtype=jnp.int32)[None, :, None]).astype(jnp.bfloat16)

    hidden = expert_hidden(gathered, route_mine.reshape(-1, 1), w_gate, w_up)
    packed = jnp.einsum("sct,sth->sch", pack, hidden.reshape(devices, rows, -1),
                        preferred_element_type=jnp.float32).astype(jnp.bfloat16)
    packed = packed.reshape(devices * cap, -1)
    if boxed:
        out = expert_out(gather_hidden(packed), w_down[0])
    else:
        groups = [list(range(h * SPLIT, (h + 1) * SPLIT)) for h in range(halves)]
        whole = lax.all_gather(packed, "local", axis=1, axis_index_groups=groups, tiled=True)
        out = jnp.dot(whole, w_down[0], preferred_element_type=jnp.float32).astype(jnp.bfloat16)
    out = jnp.einsum("sct,scd->std", pack, out.reshape(devices, cap, columns),
                     preferred_element_type=jnp.float32).astype(jnp.bfloat16)
    out = out.reshape(devices * rows, columns)
    half = lax.psum_scatter(out, "node", scatter_dimension=0, tiled=True)
    half = half.astype(jnp.bfloat16).reshape(locals_, rows, columns)
    back = lax.all_to_all(half, "local", split_axis=0, concat_axis=0, tiled=True)
    back = back.astype(jnp.float32).reshape(halves, SPLIT, rows, columns)
    mixed = jnp.sum(back, axis=0)
    return mixed.transpose(1, 0, 2).reshape(rows, width).astype(jnp.bfloat16)


def solution(mesh):
    placed = (
        P(("grp", "node", "local"), None),
        P(("grp", "node", "local"), None),
        P(("grp", "node", "local"), None),
        P(None, ("node", "local")),
        P(None, ("node", "local")),
        P(("node", "local"), None, None),
    )
    return jax.shard_map(
        on_device,
        mesh=mesh,
        in_specs=placed,
        out_specs=P(("grp", "node", "local"), None),
        check_vma=False,
    )
```
